32 devices in a mesh: groups: 2 (over y), tok: 4 (over z), col: 4 (over x, core).
Axes of the slice: x: 2, y: 2, z: 4, core: 2. Of those that a mesh axis runs over, the one named last changes fastest.
Arguments:
- attn_out: bfloat16 [512, 8192], P(('groups', 'tok'), 'col'), parts along dimension 0, may hold values from -12 to 12
- residual: bfloat16 [512, 8192], P(('groups', 'col'), 'tok'), parts along dimension 0, may hold values from -310 to 310
- w_out: bfloat16 [8192, 8192], P('col', 'tok'), may hold values from -0.0625 to 0.0625
- norm_gain: float32 [8192], P('tok'), may hold values from 0.5 to 1.5
- rotation: bfloat16 [8192, 8192], P('tok', 'col'), may hold values from -0.23201941 to 0.23201941
Outputs:
- kurtosis: float32 [512], P(('groups', 'tok')), parts along dimension 0
- grad_rot: float32 [16384, 8192], P(('groups', 'tok'), 'col'), parts along dimension 0
The draws below stay inside these ranges and needn't reach their ends.
There are 2 independent parts, one for each index of `groups`. The reference program is written for one: setup_inputs(seed, part) draws one part's arguments, and reference() takes and returns one part's arrays. A program takes and returns all parts, laid end to end along the dimension named above; an argument that names none is the same for every part. Nothing has to cross between parts.
All inputs are finite; a program needn't handle non-finite values.
Results may differ from the reference program's by a relative error of at most 0.0018.
The reference program's roundings to bfloat16 on the way count: a program that leaves them out, or rounds other values in their place, can miss the bound.
Values may be sent and summed in bfloat16 or wider, within the bound.
A program may use at most 128 MiB of HBM per device.

```python
import math
import jax
import jax.numpy as jnp
from jax import lax

D = 8192
TOKENS = 256


def draw_residual(key, part):
    key_cols = jax.random.fold_in(key, 11)
    key_rows = jax.random.fold_in(key, 12)
    key_base = jax.random.fold_in(key, 13)
    column_pos = jnp.arange(D, dtype=jnp.float32) / D
    column_scale = 0.5 * jnp.exp(math.log(3.0) * column_pos + jax.random.uniform(key_cols, (D,), jnp.float32, 0.0, math.log(3.4)))
    row_scale = jnp.exp(jax.random.uniform(key_rows, (TOKENS, 1), jnp.float32, 0.0, math.log(10.0)))
    base_draw = jnp.clip(jax.random.normal(key_base, (TOKENS, D), jnp.float32), -6.0, 6.0)
    return (base_draw * row_scale * column_scale[None, :]).astype(jnp.bfloat16)


def draw_rotation(key, part):
    key_cols = jax.random.fold_in(key, 21)
    key_base = jax.random.fold_in(key, 22)
    column_pos = jnp.arange(D, dtype=jnp.float32) / D
    column_scale = jnp.exp(math.log(3.0) * column_pos + jax.random.uniform(key_cols, (D,), jnp.float32, 0.0, math.log(3.4))) / 3.0
    base_draw = jnp.clip(jax.random.normal(key_base, (D, D), jnp.float32), -6.0, 6.0)
    return (base_draw * column_scale[None, :] / math.sqrt(D)).astype(jnp.bfloat16)


def block_scale(rng, extent, pieces, low, top_value):
    factor_of = 1.0
    for axis_at, parts in pieces:
        draws = jax.random.uniform(jax.random.fold_in(jax.random.fold_in(rng, 6), axis_at), (parts,), jnp.float32, low / len(pieces), top_value / len(pieces))
        factor_of = factor_of * jnp.repeat(jnp.exp(draws), extent[axis_at] // parts).reshape((-1,) + (1,) * (len(extent) - 1 - axis_at))
    return factor_of


def normal_values(own_key, extent, width, reach, cuts=(), kind=jnp.bfloat16):
    gain = block_scale(own_key, extent, cuts, -0.22, 0.18) if cuts else 1.0
    array = jax.random.normal(own_key, extent, jnp.float32) * width * gain
    return jnp.minimum(jnp.maximum(array, -reach), reach).astype(kind)


def setup_inputs(seed: int = 0, part: int = 0) -> dict:
    keys = jax.random.split(jax.random.key(seed), 6)
    part_keys = jax.random.split(jax.random.fold_in(keys[5], part), 6)
    return {
        "attn_out": normal_values(part_keys[0], (TOKENS, D), 2.0, 12.0, ((0, 4), (1, 4))),
        "residual": draw_residual(jax.random.fold_in(jax.random.fold_in(keys[5], part), 71), part),
        "w_out": normal_values(keys[2], (D, D), D ** -0.5, 0.0625, ((0, 4), (1, 4))),
        "norm_gain": jnp.clip(1.0 + 0.1 * jax.random.normal(keys[3], (D,), jnp.float32), 0.5, 1.5),
        "rotation": draw_rotation(jax.random.fold_in(keys[5], 71), part),
    }


norm_eps = 1e-05
moment_eps = 1e-06

def kurtosis_terms(rotated, second, fourth, full_width):
    moment_two = second / full_width + moment_eps
    kurt_vals = fourth / full_width / (moment_two * moment_two)
    cubed = rotated * rotated * rotated
    grad_vals = cubed / (moment_two * moment_two)[:, None] - (kurt_vals / moment_two)[:, None] * rotated
    return (kurt_vals, grad_vals.astype(jnp.bfloat16))

def reference(attn_out, residual, w_out, norm_gain, rotation):
    projected = jnp.dot(attn_out, w_out, preferred_element_type=jnp.float32)
    hidden = residual.astype(jnp.float32) + projected
    square_sum = lax.optimization_barrier(jnp.sum(hidden * hidden, axis=1))
    row_scale = lax.rsqrt(square_sum / D + norm_eps)
    normed = (hidden * row_scale[:, None] * norm_gain[None, :]).astype(jnp.bfloat16)
    rotated = jnp.dot(normed, rotation, preferred_element_type=jnp.float32)
    squares = rotated * rotated
    second = lax.optimization_barrier(jnp.sum(squares, axis=1))
    fourth = lax.optimization_barrier(jnp.sum(squares * squares, axis=1))
    kurt_vals, grad_vals = kurtosis_terms(rotated, second, fourth, D)
    grad_rot = lax.dot_general(normed, grad_vals, (((0,), (0,)), ((), ())), preferred_element_type=jnp.float32)
    return (kurt_vals, grad_rot / math.sqrt(TOKENS))
```

```python
import functools
import math

import jax
import jax.numpy as jnp
from jax import lax
from jax.experimental import pallas as pl
from jax.experimental.pallas import tpu as pltpu
from jax.sharding import PartitionSpec as P

norm_eps = 1e-05
moment_eps = 1e-06


def kurtosis_terms(rotated, second, fourth, full_width):
    moment_two = second / full_width + moment_eps
    kurt_vals = fourth / full_width / (moment_two * moment_two)
    cubed = rotated * rotated * rotated
    grad_vals = (
        cubed / (moment_two * moment_two)[:, None] - (kurt_vals / moment_two)[:, None] * rotated
    )
    return (kurt_vals, grad_vals.astype(jnp.bfloat16))


def power_sums(rotated, along):
    squares = rotated * rotated
    return (jnp.sum(squares, axis=along), jnp.sum(squares * squares, axis=along))


def shards(attn_out, residual, w_out, norm_gain, rotation):
    heads_all = lax.all_gather(attn_out, "tok", axis=0, tiled=True)
    row_block = heads_all
    projected = lax.psum_scatter(
        jnp.dot(row_block, w_out, preferred_element_type=jnp.float32),
        "col",
        scatter_dimension=0,
        tiled=True,
    )
    hidden = residual.astype(jnp.float32) + projected
    square_sum = lax.psum(jnp.sum(hidden * hidden, axis=1), "tok")
    full_width = hidden.shape[1] * lax.axis_size("tok")
    row_scale = lax.rsqrt(square_sum / full_width + norm_eps)
    normed = (hidden * row_scale[:, None] * norm_gain[None, :]).astype(jnp.bfloat16)
    normed_all = lax.all_gather(normed, "col", axis=0, tiled=True)
    tokens_total = normed_all.shape[0]
    row_block = normed_all
    rotated = lax.psum_scatter(
        jnp.dot(row_block, rotation, preferred_element_type=jnp.float32),
        "tok",
        scatter_dimension=0,
        tiled=True,
    )
    second, fourth = lax.psum(power_sums(rotated, 1), "col")
    kurt_vals, grad_own = kurtosis_terms(rotated, second, fourth, full_width)
    grad_all = lax.all_gather(grad_own, "tok", axis=0, tiled=True)
    grad_rot = lax.dot_general(
        normed_all, grad_all, (((0,), (0,)), ((), ())), preferred_element_type=jnp.float32
    )
    return (kurt_vals, grad_rot / math.sqrt(tokens_total))


MESH = pl.DeviceIdType.MESH
block_order = (0, 2, 1, 3)
tile_cols = 256
row_step = 16


def rows_loop(count, body):
    def step(i, carry):
        body(pl.ds(pl.multiple_of(i * row_step, row_step), row_step))
        return carry

    lax.fori_loop(0, count // row_step, step, 0)


def kernel(
    full_width,
    attn_ref, res_ref, gain_ref, w_hbm, rot_hbm,
    kurt_ref, norm_ref, grad_ref,
    attn_all, w, rot, part, mate_buf, x_buf, rotp, z_buf, sumsq, stats,
    load_sem, ag_send, ag_recv, m_send, m_recv, x_send, x_recv, ss_send, ss_recv,
    n_send, n_recv, z_send, z_recv, st_send, st_recv, g_send, g_recv, k_send, k_recv, k_local,
):
    g = lax.axis_index("groups")
    z = lax.axis_index("tok")
    c = lax.axis_index("col")
    core = lax.rem(c, 2)
    chip = lax.div(c, 2)
    mate = c + 1 - 2 * core
    across = lax.rem(c + 2, 4)
    block, width = attn_ref.shape
    half = block // 2

    def remote(src, dst, send, recv, to_z, to_c):
        return pltpu.make_async_remote_copy(
            src_ref=src, dst_ref=dst, send_sem=send, recv_sem=recv,
            device_id=(g, to_z, to_c), device_id_type=MESH,
        )

    load_w = pltpu.make_async_copy(w_hbm, w, load_sem.at[0])
    load_rot = pltpu.make_async_copy(rot_hbm, rot, load_sem.at[1])
    load_w.start()

    barrier = pltpu.get_barrier_semaphore()
    for d in (1, 2, 3):
        pl.semaphore_signal(barrier, inc=1, device_id=(g, lax.rem(z + d, 4), c), device_id_type=MESH)
        pl.semaphore_signal(barrier, inc=1, device_id=(g, z, lax.rem(c + d, 4)), device_id_type=MESH)
    attn_all[z] = attn_ref[...]
    pl.semaphore_wait(barrier, 6)

    above = jnp.minimum(z + 1, 3)
    below = jnp.maximum(z - 1, 0)
    is_end = (z == 0) | (z == 3)
    is_mid = jnp.logical_not(is_end)

    def ag(s, up):
        return remote(
            attn_all.at[s], attn_all.at[s], ag_send.at[up, s], ag_recv.at[s],
            above if up else below, c,
        )

    def when(cond):
        return pl.when(cond)

    @when(z < 3)
    def _():
        ag(z, 1).start()

    @when(z > 0)
    def _():
        ag(z, 0).start()

    def tiles(left, left_at, right, out):
        def step(i, carry):
            cols = pl.ds(pl.multiple_of(i * tile_cols, tile_cols), tile_cols)
            out[left_at, :, cols] = jnp.dot(
                left[left_at], right[:, cols], preferred_element_type=jnp.float32
            )
            return carry

        lax.fori_loop(0, width // tile_cols, step, 0)

    def mate_copy(s):
        return remote(
            part.at[s], mate_buf.at[lax.div(s, 2)], m_send.at[lax.div(s, 2)],
            m_recv.at[lax.div(s, 2)], z, mate,
        )

    def x_copy(s):
        return remote(part.at[s], x_buf, x_send.at[0], x_recv.at[0], z, across)

    def project(s):
        tiles(attn_all, s, w, part)

        @when(lax.rem(s, 2) != core)
        def _():
            mate_copy(s).start()

    def pair_sum(s):
        @when(lax.rem(s, 2) == core)
        def _():
            at = lax.div(s, 2)
            mate_copy(s).wait_recv()

            def add(rows):
                part[s, rows, :] += mate_buf[at, rows, :]

            rows_loop(block, add)

            @when(at != chip)
            def _():
                x_copy(s).start()

    first = jnp.where(z == 0, 1, z - 1)
    second = jnp.where(z == 0, 2, jnp.where(z == 3, 1, z + 1))
    third = jnp.where(z < 2, 3, 0)
    two_away = jnp.where(z < 2, z + 2, z - 2)

    load_w.wait()
    load_rot.start()
    project(z)

    @when(z > 0)
    def _():
        ag(below, 1).wait_recv()

        @when(z < 3)
        def _():
            ag(below, 1).start()

    @when(z < 3)
    def _():
        ag(above, 0).wait_recv()

        @when(z > 0)
        def _():
            ag(above, 0).start()

    project(first)
    pair_sum(z)
    ag(two_away, 0).wait_recv()

    @when(z == 1)
    def _():
        ag(two_away, 0).start()

    @when(z == 2)
    def _():
        ag(two_away, 1).start()

    project(second)
    pair_sum(first)

    @when(is_end)
    def _():
        ag(third, 0).wait_recv()

    project(third)
    pair_sum(second)
    pair_sum(third)

    x_copy(c).wait_recv()

    def add_residual(rows):
        hidden = res_ref[rows, :].astype(jnp.float32) + (part[c, rows, :] + x_buf[rows, :])
        part[c, rows, :] = hidden
        sumsq[z, rows, :] = jnp.broadcast_to(
            jnp.sum(hidden * hidden, axis=1, keepdims=True), (row_step, 128)
        )

    rows_loop(block, add_residual)

    def ss_copy(to_z):
        return remote(sumsq.at[z], sumsq.at[z], ss_send.at[to_z], ss_recv.at[z], to_z, c)

    def ss_arrival(from_z):
        return remote(
            sumsq.at[from_z], sumsq.at[from_z], ss_send.at[from_z], ss_recv.at[from_z], from_z, c
        )

    for d in (1, 2, 3):
        ss_copy(lax.rem(z + d, 4)).start()
    for d in (1, 2, 3):
        ss_arrival(lax.rem(z + d, 4)).wait_recv()

    def normalise(rows):
        total = sumsq[0, rows, :] + sumsq[1, rows, :] + sumsq[2, rows, :] + sumsq[3, rows, :]
        scale = lax.rsqrt(total / full_width + norm_eps)[:, :1]
        norm_ref[c, rows, :] = (part[c, rows, :] * scale * gain_ref[...]).astype(jnp.bfloat16)

    rows_loop(block, normalise)

    def norm_copy(b, at, to_c):
        return remote(norm_ref.at[b], norm_ref.at[b], n_send.at[at], n_recv.at[b], z, to_c)

    norm_copy(c, 0, across).start()
    norm_copy(c, 1, mate).start()
    load_rot.wait()

    def rotate(b):
        @when(c != b)
        def _():
            norm_copy(b, 0, mate).wait_recv()

        @when(across == b)
        def _():
            norm_copy(b, 2, mate).start()

        tiles(norm_ref, b, rot, rotp)

    def z_copy(b, h, to_z):
        piece = pl.ds(pl.multiple_of(h * half, half), half)
        return remote(
            rotp.at[b, piece], z_buf.at[b, h], z_send.at[b, h], z_recv.at[b, h], to_z, c
        )

    def g_copy(b, h, to_z):
        piece = pl.ds(pl.multiple_of(h * half, half), half)
        return remote(
            grad_ref.at[b, piece], grad_ref.at[b, piece], g_send.at[b, h], g_recv.at[b, h], to_z, c
        )

    def chain_add(b, h):
        z_copy(b, h, below).wait_recv()

        def add(i, carry):
            here = pl.ds(pl.multiple_of(i * row_step, row_step), row_step)
            there = pl.ds(pl.multiple_of(h * half + i * row_step, row_step), row_step)
            rotp[b, there, :] += z_buf[b, h, here, :]
            return carry

        lax.fori_loop(0, half // row_step, add, 0)

    out_half = jnp.where(z == 0, 1, 0)
    in_half = 1 - out_half
    inner = jnp.where(z == 0, 1, 2)
    near = jnp.where(z == 1, 1, 0)
    far = 1 - near
    end_z = jnp.where(z == 1, 0, 3)
    other_mid = jnp.where(z == 1, 2, 1)

    def near_step(b):
        chain_add(b, near)
        z_copy(b, near, other_mid).start()

    def far_step(b):
        chain_add(b, far)
        z_copy(b, far, end_z).start()

    b0, b1, b2, b3 = block_order

    def stat_copy(b, to_c):
        return remote(stats.at[b, c], stats.at[b, c], st_send.at[b, to_c], st_recv.at[b, c], z, to_c)

    def stat_arrival(b, from_c):
        return remote(
            stats.at[b, from_c], stats.at[b, from_c], st_send.at[b, from_c], st_recv.at[b, from_c],
            z, from_c,
        )

    def kurt_copy(b):
        return remote(
            stats.at[b, 4, 0], kurt_ref.at[in_half], k_send.at[b], k_recv.at[in_half],
            jnp.int32(b), c,
        )

    def finish(b):
        chain_add(b, in_half)

        def moments(i, carry):
            here = pl.ds(pl.multiple_of(i * row_step, row_step), row_step)
            there = pl.ds(pl.multiple_of(in_half * half + i * row_step, row_step), row_step)
            squares = rotp[b, there, :]
            squares = squares * squares
            stats[b, c, 0, here, :] = jnp.broadcast_to(
                jnp.sum(squares, axis=1, keepdims=True), (row_step, 128)
            )
            stats[b, c, 1, here, :] = jnp.broadcast_to(
                jnp.sum(squares * squares, axis=1, keepdims=True), (row_step, 128)
            )
            return carry

        lax.fori_loop(0, half // row_step, moments, 0)
        for d in (1, 2, 3):
            stat_copy(b, lax.rem(c + d, 4)).start()
        for d in (1, 2, 3):
            stat_arrival(b, lax.rem(c + d, 4)).wait_recv()

        def grads(i, carry):
            here = pl.ds(pl.multiple_of(i * row_step, row_step), row_step)
            there = pl.ds(pl.multiple_of(in_half * half + i * row_step, row_step), row_step)
            sums = [
                stats[b, 0, q, here, :] + stats[b, 1, q, here, :]
                + stats[b, 2, q, here, :] + stats[b, 3, q, here, :]
                for q in (0, 1)
            ]
            moment = sums[0] / full_width + moment_eps
            squared = moment * moment
            kurt = sums[1] / full_width / squared
            stats[b, 4, 0, here, :] = kurt
            cubic = (1.0 / squared)[:, :1]
            linear = (kurt / moment)[:, :1]
            rotated = rotp[b, there, :]
            grad_ref[b, there, :] = (
                rotated * rotated * rotated * cubic - linear * rotated
            ).astype(jnp.bfloat16)
            return carry

        lax.fori_loop(0, half // row_step, grads, 0)
        g_copy(b, in_half, inner).start()

        @when(z != b)
        def _():
            kurt_copy(b).start()

        if b in (0, 3):

            @when(z == b)
            def _():
                own = pltpu.make_async_copy(stats.at[b, 4, 0], kurt_ref.at[in_half], k_local.at[0])
                own.start()
                own.wait()

    def near_grad(b):
        g_copy(b, far, other_mid).wait_recv()
        g_copy(b, far, other_mid).start()

    def far_grad(b):
        g_copy(b, near, end_z).wait_recv()
        g_copy(b, near, end_z).start()

    @when(is_end)
    def _():
        for b in block_order:
            rotate(b)
            z_copy(b, out_half, inner).start()
        for b in block_order:
            finish(b)
        for b in block_order:
            g_copy(b, out_half, inner).wait_recv()

    @when(is_mid)
    def _():
        rotate(b0)
        rotate(b1)
        near_step(b0)
        rotate(b2)
        near_step(b1)
        far_step(b0)
        rotate(b3)
        near_step(b2)
        far_step(b1)
        near_step(b3)
        far_step(b2)
        far_step(b3)
        near_grad(b0)
        for at in (1, 2, 3):
            near_grad(block_order[at])
            far_grad(block_order[at - 1])
        far_grad(b3)

    def kurt_arrival(h):
        return remote(
            stats.at[0, 4, 0], kurt_ref.at[h], k_send.at[0], k_recv.at[h], jnp.int32(3 * h), c
        )

    @when(z != 0)
    def _():
        kurt_arrival(0).wait_recv()

    @when(z != 3)
    def _():
        kurt_arrival(1).wait_recv()

    for s in range(4):

        @when((s <= z) & (z < 3))
        def _():
            ag(s, 1).wait_send()

        @when((s >= z) & (z > 0))
        def _():
            ag(s, 0).wait_send()

        @when(core != s % 2)
        def _():
            mate_copy(jnp.int32(s)).wait_send()

        @when(is_mid)
        def _():
            for h in (0, 1):
                z_copy(s, h, below).wait_send()
                g_copy(s, h, below).wait_send()

        @when(is_end)
        def _():
            z_copy(s, out_half, inner).wait_send()
            g_copy(s, in_half, inner).wait_send()
            for d in (1, 2, 3):
                stat_copy(s, lax.rem(c + d, 4)).wait_send()

            @when(z != s)
            def _():
                kurt_copy(s).wait_send()

    x_copy(across).wait_send()
    for d in (1, 2, 3):
        ss_copy(lax.rem(z + d, 4)).wait_send()
    norm_copy(c, 0, across).wait_send()
    norm_copy(c, 1, mate).wait_send()
    norm_copy(across, 2, mate).wait_send()


def fused_shards(attn_out, residual, w_out, norm_gain, rotation):
    block, width = attn_out.shape
    full_width = width * 4
    half = block // 2
    dma = pltpu.SemaphoreType.DMA
    vmem = pl.BlockSpec(memory_space=pltpu.VMEM)
    kurt, normed, grads = pl.pallas_call(
        functools.partial(kernel, full_width),
        out_shape=(
            jax.ShapeDtypeStruct((2, half, 128), jnp.float32),
            jax.ShapeDtypeStruct((4, block, width), jnp.bfloat16),
            jax.ShapeDtypeStruct((4, block, width), jnp.bfloat16),
        ),
        in_specs=[vmem, vmem, vmem, pl.BlockSpec(memory_space=pl.ANY), pl.BlockSpec(memory_space=pl.ANY)],
        out_specs=(vmem, vmem, vmem),
        scratch_shapes=[
            pltpu.VMEM((4, block, width), jnp.bfloat16),
            pltpu.VMEM(w_out.shape, jnp.bfloat16),
            pltpu.VMEM(rotation.shape, jnp.bfloat16),
            pltpu.VMEM((4, block, width), jnp.float32),
            pltpu.VMEM((2, block, width), jnp.float32),
            pltpu.VMEM((block, width), jnp.float32),
            pltpu.VMEM((4, block, width), jnp.float32),
            pltpu.VMEM((4, 2, half, width), jnp.float32),
            pltpu.VMEM((4, block, 128), jnp.float32),
            pltpu.VMEM((4, 5, 2, half, 128), jnp.float32),
            dma((2,)), dma((2, 4)), dma((4,)), dma((2,)), dma((2,)), dma((1,)), dma((1,)),
            dma((4,)), dma((4,)), dma((3,)), dma((4,)), dma((4, 2)), dma((4, 2)),
            dma((4, 4)), dma((4, 4)), dma((4, 2)), dma((4, 2)), dma((4,)), dma((2,)), dma((1,)),
        ],
        compiler_params=pltpu.CompilerParams(
            collective_id=0, has_side_effects=True, vmem_limit_bytes=48 * 1024 * 1024
        ),
    )(attn_out, residual, norm_gain.reshape(1, width), w_out, rotation)
    normed = normed.reshape(4 * block, width)
    grads = grads.reshape(4 * block, width)
    grad_rot = lax.dot_general(
        normed, grads, (((0,), (0,)), ((), ())), preferred_element_type=jnp.float32
    )
    return (kurt[:, :, 0].reshape(block), grad_rot / math.sqrt(4 * block))


def solution(mesh):
    fits = mesh.shape["tok"] == 4 and mesh.shape["col"] == 4
    return jax.shard_map(
        fused_shards if fits else shards,
        mesh=mesh,
        in_specs=(
            P(("groups", "tok"), "col"),
            P(("groups", "col"), "tok"),
            P("col", "tok"),
            P("tok"),
            P("tok", "col"),
        ),
        out_specs=(P(("groups", "tok")), P(("groups", "tok"), "col")),
        check_vma=False,
    )
```

```python
import functools
import math

import jax
import jax.numpy as jnp
from jax import lax
from jax.experimental import pallas as pl
from jax.experimental.pallas import tpu as pltpu
from jax.sharding import PartitionSpec as P

norm_eps = 1e-05
moment_eps = 1e-06


def kurtosis_terms(rotated, second, fourth, full_width):
    moment_two = second / full_width + moment_eps
    kurt_vals = fourth / full_width / (moment_two * moment_two)
    cubed = rotated * rotated * rotated
    grad_vals = (
        cubed / (moment_two * moment_two)[:, None] - (kurt_vals / moment_two)[:, None] * rotated
    )
    return (kurt_vals, grad_vals.astype(jnp.bfloat16))


def power_sums(rotated, along):
    squares = rotated * rotated
    return (jnp.sum(squares, axis=along), jnp.sum(squares * squares, axis=along))


def shards(attn_out, residual, w_out, norm_gain, rotation):
    heads_all = lax.all_gather(attn_out, "tok", axis=0, tiled=True)
    row_block = heads_all
    projected = lax.psum_scatter(
        jnp.dot(row_block, w_out, preferred_element_type=jnp.float32),
        "col",
        scatter_dimension=0,
        tiled=True,
    )
    hidden = residual.astype(jnp.float32) + projected
    square_sum = lax.psum(jnp.sum(hidden * hidden, axis=1), "tok")
    full_width = hidden.shape[1] * lax.axis_size("tok")
    row_scale = lax.rsqrt(square_sum / full_width + norm_eps)
    normed = (hidden * row_scale[:, None] * norm_gain[None, :]).astype(jnp.bfloat16)
    normed_all = lax.all_gather(normed, "col", axis=0, tiled=True)
    tokens_total = normed_all.shape[0]
    row_block = normed_all
    rotated = lax.psum_scatter(
        jnp.dot(row_block, rotation, preferred_element_type=jnp.float32),
        "tok",
        scatter_dimension=0,
        tiled=True,
    )
    second, fourth = lax.psum(power_sums(rotated, 1), "col")
    kurt_vals, grad_own = kurtosis_terms(rotated, second, fourth, full_width)
    grad_all = lax.all_gather(grad_own, "tok", axis=0, tiled=True)
    grad_rot = lax.dot_general(
        normed_all, grad_all, (((0,), (0,)), ((), ())), preferred_element_type=jnp.float32
    )
    return (kurt_vals, grad_rot / math.sqrt(tokens_total))


MESH = pl.DeviceIdType.MESH
block_order = (0, 2, 1, 3)
tile_cols = 256
row_step = 16


def rows_loop(count, body):
    def step(i, carry):
        body(pl.ds(pl.multiple_of(i * row_step, row_step), row_step))
        return carry

    lax.fori_loop(0, count // row_step, step, 0)


def kernel(
    full_width,
    attn_hbm, res_hbm, gain_hbm, w_hbm, rot_hbm,
    kurt_ref, norm_ref, grad_ref,
    res_ref, gain_ref, attn_all, w, rot, part, mate_buf, x_buf, rotp, z_buf, sumsq, stats,
    load_sem, ag_send, ag_recv, m_send, m_recv, x_send, x_recv, ss_send, ss_recv,
    n_send, n_recv, z_send, z_recv, st_send, st_recv, g_send, g_recv, k_send, k_recv,
):
    g = lax.axis_index("groups")
    z = lax.axis_index("tok")
    c = lax.axis_index("col")
    core = lax.rem(c, 2)
    chip = lax.div(c, 2)
    mate = c + 1 - 2 * core
    across = lax.rem(c + 2, 4)
    block, width = attn_hbm.shape
    half = block // 2
    quarter = half // 2
    half_cols = width // 2

    def remote(src, dst, send, recv, to_z, to_c):
        return pltpu.make_async_remote_copy(
            src_ref=src, dst_ref=dst, send_sem=send, recv_sem=recv,
            device_id=(g, to_z, to_c), device_id_type=MESH,
        )

    def side(q):
        return pl.ds(q * half_cols, half_cols)

    load_attn = pltpu.make_async_copy(attn_hbm, attn_all.at[z], load_sem.at[0])
    load_w = [
        pltpu.make_async_copy(w_hbm.at[:, side(q)], w.at[:, side(q)], load_sem.at[1 + q])
        for q in (0, 1)
    ]
    load_rot = pltpu.make_async_copy(rot_hbm, rot, load_sem.at[3])
    load_res = pltpu.make_async_copy(res_hbm, res_ref, load_sem.at[4])
    load_gain = pltpu.make_async_copy(gain_hbm, gain_ref, load_sem.at[5])
    load_attn.start()
    load_w[0].start()
    load_w[1].start()

    barrier = pltpu.get_barrier_semaphore()
    for d in (1, 2, 3):
        pl.semaphore_signal(barrier, inc=1, device_id=(g, lax.rem(z + d, 4), c), device_id_type=MESH)
        pl.semaphore_signal(barrier, inc=1, device_id=(g, z, lax.rem(c + d, 4)), device_id_type=MESH)
    pl.semaphore_wait(barrier, 6)

    above = jnp.minimum(z + 1, 3)
    below = jnp.maximum(z - 1, 0)
    is_end = (z == 0) | (z == 3)
    is_mid = jnp.logical_not(is_end)

    def ag(s, up):
        return remote(
            attn_all.at[s], attn_all.at[s], ag_send.at[up, s], ag_recv.at[s],
            above if up else below, c,
        )

    def when(cond):
        return pl.when(cond)

    def ag_own(up):
        return remote(
            attn_hbm, attn_all.at[z], ag_send.at[up, z], ag_recv.at[z],
            above if up else below, c,
        )

    @when(z < 3)
    def _():
        ag_own(1).start()

    @when(z > 0)
    def _():
        ag_own(0).start()

    def tiles(left, left_at, right, out, q):
        def step(i, carry):
            cols = pl.ds(pl.multiple_of(q * half_cols + i * tile_cols, tile_cols), tile_cols)
            out[left_at, :, cols] = jnp.dot(
                left[left_at], right[:, cols], preferred_element_type=jnp.float32
            )
            return carry

        lax.fori_loop(0, half_cols // tile_cols, step, 0)

    def mate_copy(s, q):
        at = lax.div(s, 2)
        return remote(
            part.at[s, :, side(q)], mate_buf.at[at, :, side(q)], m_send.at[at, q],
            m_recv.at[at, q], z, mate,
        )

    def x_copy(s, q):
        return remote(
            part.at[s, :, side(q)], x_buf.at[:, side(q)], x_send.at[q], x_recv.at[q], z, across
        )

    def project(s, q):
        tiles(attn_all, s, w, part, q)

        @when(lax.rem(s, 2) != core)
        def _():
            mate_copy(s, q).start()

    def pair_sum(s, q):
        @when(lax.rem(s, 2) == core)
        def _():
            at = lax.div(s, 2)
            mate_copy(s, q).wait_recv()

            def add(rows):
                part[s, rows, side(q)] += mate_buf[at, rows, side(q)]

            rows_loop(block, add)

            @when(at != chip)
            def _():
                x_copy(s, q).start()

    first = jnp.where(z == 0, 1, z - 1)
    second = jnp.where(z == 0, 2, jnp.where(z == 3, 1, z + 1))
    third = jnp.where(z < 2, 3, 0)
    two_away = jnp.where(z < 2, z + 2, z - 2)

    load_attn.wait()
    load_w[0].wait()
    load_rot.start()
    load_res.start()
    load_gain.start()
    project(z, 0)

    @when(z > 0)
    def _():
        ag(below, 1).wait_recv()

        @when(z < 3)
        def _():
            ag(below, 1).start()

    @when(z < 3)
    def _():
        ag(above, 0).wait_recv()

        @when(z > 0)
        def _():
            ag(above, 0).start()

    load_w[1].wait()
    project(z, 1)
    pair_sum(z, 0)
    project(first, 0)
    pair_sum(z, 1)
    project(first, 1)
    pair_sum(first, 0)
    ag(two_away, 0).wait_recv()

    @when(z == 1)
    def _():
        ag(two_away, 0).start()

    @when(z == 2)
    def _():
        ag(two_away, 1).start()

    project(second, 0)
    pair_sum(first, 1)
    project(second, 1)
    pair_sum(second, 0)

    @when(is_end)
    def _():
        pair_sum(second, 1)
        ag(third, 0).wait_recv()

    project(third, 0)

    @when(is_mid)
    def _():
        pair_sum(second, 1)

    project(third, 1)
    pair_sum(third, 0)
    pair_sum(third, 1)

    load_res.wait()
    load_gain.wait()
    x_copy(c, 0).wait_recv()
    x_copy(c, 1).wait_recv()

    def add_residual(rows):
        hidden = res_ref[rows, :].astype(jnp.float32) + (part[c, rows, :] + x_buf[rows, :])
        part[c, rows, :] = hidden
        sumsq[z, rows, :] = jnp.broadcast_to(
            jnp.sum(hidden * hidden, axis=1, keepdims=True), (row_step, 128)
        )

    rows_loop(block, add_residual)

    def ss_copy(to_z):
        return remote(sumsq.at[z], sumsq.at[z], ss_send.at[to_z], ss_recv.at[z], to_z, c)

    def ss_arrival(from_z):
        return remote(
            sumsq.at[from_z], sumsq.at[from_z], ss_send.at[from_z], ss_recv.at[from_z], from_z, c
        )

    for d in (1, 2, 3):
        ss_copy(lax.rem(z + d, 4)).start()
    for d in (1, 2, 3):
        ss_arrival(lax.rem(z + d, 4)).wait_recv()

    def normalise(rows):
        total = sumsq[0, rows, :] + sumsq[1, rows, :] + sumsq[2, rows, :] + sumsq[3, rows, :]
        scale = lax.rsqrt(total / full_width + norm_eps)[:, :1]
        norm_ref[c, rows, :] = (part[c, rows, :] * scale * gain_ref[...]).astype(jnp.bfloat16)

    rows_loop(block, normalise)

    def norm_copy(b, at, to_c):
        return remote(norm_ref.at[b], norm_ref.at[b], n_send.at[at], n_recv.at[b], z, to_c)

    norm_copy(c, 0, across).start()
    norm_copy(c, 1, mate).start()
    load_rot.wait()

    def rotate(b, q):
        if q == 0:

            @when(c != b)
            def _():
                norm_copy(b, 0, mate).wait_recv()

            @when(across == b)
            def _():
                norm_copy(b, 2, mate).start()

        tiles(norm_ref, b, rot, rotp, q)

    def piece(h, q):
        return pl.ds(pl.multiple_of(h * half + q * quarter, quarter), quarter)

    def z_copy(u, h, to_z):
        b, q = u
        return remote(
            rotp.at[b, piece(h, q)], z_buf.at[b, h, q], z_send.at[b, h, q], z_recv.at[b, h, q],
            to_z, c,
        )

    def g_copy(u, h, to_z):
        b, q = u
        return remote(
            grad_ref.at[b, piece(h, q)], grad_ref.at[b, piece(h, q)], g_send.at[b, h, q],
            g_recv.at[b, h, q], to_z, c,
        )

    def chain_add(u, h):
        b, q = u
        z_copy(u, h, below).wait_recv()
        rotp[b, piece(h, q), :] += z_buf[b, h, q]

    out_half = jnp.where(z == 0, 1, 0)
    in_half = 1 - out_half
    inner = jnp.where(z == 0, 1, 2)
    near = jnp.where(z == 1, 1, 0)
    far = 1 - near
    end_z = jnp.where(z == 1, 0, 3)
    other_mid = jnp.where(z == 1, 2, 1)
    units = [(b, q) for b in block_order for q in (0, 1)]
    last = len(units)

    def near_step(i):
        if 0 <= i < last:
            chain_add(units[i], near)
            z_copy(units[i], near, other_mid).start()

    def far_step(i):
        if 0 <= i < last:
            chain_add(units[i], far)
            z_copy(units[i], far, end_z).start()

    def stat_copy(u, to_c):
        b, q = u
        return remote(
            stats.at[b, q, c], stats.at[b, q, c], st_send.at[b, q, to_c], st_recv.at[b, q, c],
            z, to_c,
        )

    def stat_arrival(u, from_c):
        b, q = u
        return remote(
            stats.at[b, q, from_c], stats.at[b, q, from_c], st_send.at[b, q, from_c],
            st_recv.at[b, q, from_c], z, from_c,
        )

    def kurt_copy(u):
        b, q = u
        return remote(
            stats.at[b, q, 4, 0], kurt_ref.at[in_half, q], k_send.at[b, q], k_recv.at[in_half, q],
            jnp.int32(b), c,
        )

    def moments(u):
        b, q = u
        chain_add(u, in_half)
        squares = rotp[b, piece(in_half, q), :]
        squares = squares * squares
        stats[b, q, c, 0] = jnp.broadcast_to(
            jnp.sum(squares, axis=1, keepdims=True), (quarter, 128)
        )
        stats[b, q, c, 1] = jnp.broadcast_to(
            jnp.sum(squares * squares, axis=1, keepdims=True), (quarter, 128)
        )
        for d in (1, 2, 3):
            stat_copy(u, lax.rem(c + d, 4)).start()

    def finish(u):
        b, q = u
        for d in (1, 2, 3):
            stat_arrival(u, lax.rem(c + d, 4)).wait_recv()
        sums = [
            stats[b, q, 0, p] + stats[b, q, 1, p] + stats[b, q, 2, p] + stats[b, q, 3, p]
            for p in (0, 1)
        ]
        moment = sums[0] / full_width + moment_eps
        squared = moment * moment
        kurt = sums[1] / full_width / squared
        stats[b, q, 4, 0] = kurt
        cubic = (1.0 / squared)[:, :1]
        linear = (kurt / moment)[:, :1]
        rotated = rotp[b, piece(in_half, q), :]
        grad_ref[b, piece(in_half, q), :] = (
            rotated * rotated * rotated * cubic - linear * rotated
        ).astype(jnp.bfloat16)
        g_copy(u, in_half, inner).start()

        @when(z != b)
        def _():
            kurt_copy(u).start()

        if b in (0, 3):

            @when(z == b)
            def _():
                kurt_ref[in_half, q] = kurt

    def near_grad(i):
        if 0 <= i < last:
            g_copy(units[i], far, other_mid).wait_recv()
            g_copy(units[i], far, other_mid).start()

    def far_grad(i):
        if 0 <= i < last:
            g_copy(units[i], near, end_z).wait_recv()
            g_copy(units[i], near, end_z).start()

    @when(is_end)
    def _():
        for b in block_order:
            rotate(b, 0)
            rotate(b, 1)
            for q in (0, 1):
                z_copy((b, q), out_half, inner).start()
        for i, u in enumerate(units):
            moments(u)
            if i > 0:
                finish(units[i - 1])
        finish(units[-1])
        for u in units:
            g_copy(u, out_half, inner).wait_recv()

    @when(is_mid)
    def _():
        for b in block_order[:2]:
            rotate(b, 0)
            rotate(b, 1)
        later = [(b, q) for b in block_order[2:] for q in (0, 1)]
        for i in range(last + 8):
            near_step(i)
            far_step(i - 1)
            near_grad(i - 6)
            far_grad(i - 7)
            if i < len(later):
                rotate(*later[i])

    def kurt_arrival(h, q):
        return remote(
            stats.at[0, q, 4, 0], kurt_ref.at[h, q], k_send.at[0, q], k_recv.at[h, q],
            jnp.int32(3 * h), c,
        )

    for q in (0, 1):

        @when(z != 0)
        def _():
            kurt_arrival(0, q).wait_recv()

        @when(z != 3)
        def _():
            kurt_arrival(1, q).wait_recv()

    for s in range(4):

        @when((s <= z) & (z < 3))
        def _():
            ag(s, 1).wait_send()

        @when((s >= z) & (z > 0))
        def _():
            ag(s, 0).wait_send()

        for q in (0, 1):

            @when(core != s % 2)
            def _():
                mate_copy(jnp.int32(s), q).wait_send()

            u = (s, q)

            @when(is_mid)
            def _():
                for h in (0, 1):
                    z_copy(u, h, below).wait_send()
                    g_copy(u, h, below).wait_send()

            @when(is_end)
            def _():
                z_copy(u, out_half, inner).wait_send()
                g_copy(u, in_half, inner).wait_send()
                for d in (1, 2, 3):
                    stat_copy(u, lax.rem(c + d, 4)).wait_send()

                @when(z != s)
                def _():
                    kurt_copy(u).wait_send()

    for q in (0, 1):
        x_copy(across, q).wait_send()
    for d in (1, 2, 3):
        ss_copy(lax.rem(z + d, 4)).wait_send()
    norm_copy(c, 0, across).wait_send()
    norm_copy(c, 1, mate).wait_send()
    norm_copy(across, 2, mate).wait_send()


def fused_shards(attn_out, residual, w_out, norm_gain, rotation):
    block, width = attn_out.shape
    full_width = width * 4
    quarter = block // 4
    dma = pltpu.SemaphoreType.DMA
    vmem = pl.BlockSpec(memory_space=pltpu.VMEM)
    kurt, normed, grads = pl.pallas_call(
        functools.partial(kernel, full_width),
        out_shape=(
            jax.ShapeDtypeStruct((2, 2, quarter, 128), jnp.float32),
            jax.ShapeDtypeStruct((4, block, width), jnp.bfloat16),
            jax.ShapeDtypeStruct((4, block, width), jnp.bfloat16),
        ),
        in_specs=[pl.BlockSpec(memory_space=pltpu.HBM)] * 5,
        out_specs=(vmem, vmem, vmem),
        scratch_shapes=[
            pltpu.VMEM((block, width), jnp.bfloat16),
            pltpu.VMEM((1, width), jnp.float32),
            pltpu.VMEM((4, block, width), jnp.bfloat16),
            pltpu.VMEM(w_out.shape, jnp.bfloat16),
            pltpu.VMEM(rotation.shape, jnp.bfloat16),
            pltpu.VMEM((4, block, width), jnp.float32),
            pltpu.VMEM((2, block, width), jnp.float32),
            pltpu.VMEM((block, width), jnp.float32),
            pltpu.VMEM((4, block, width), jnp.float32),
            pltpu.VMEM((4, 2, 2, quarter, width), jnp.float32),
            pltpu.VMEM((4, block, 128), jnp.float32),
            pltpu.VMEM((4, 2, 5, 2, quarter, 128), jnp.float32),
            dma((6,)), dma((2, 4)), dma((4,)), dma((2, 2)), dma((2, 2)), dma((2,)), dma((2,)),
            dma((4,)), dma((4,)), dma((3,)), dma((4,)), dma((4, 2, 2)), dma((4, 2, 2)),
            dma((4, 2, 4)), dma((4, 2, 4)), dma((4, 2, 2)), dma((4, 2, 2)), dma((4, 2)), dma((2, 2)),
        ],
        compiler_params=pltpu.CompilerParams(
            collective_id=0, has_side_effects=True, vmem_limit_bytes=60 * 1024 * 1024
        ),
    )(attn_out, residual, norm_gain.reshape(1, width), w_out, rotation)
    normed = normed.reshape(4 * block, width)
    grads = grads.reshape(4 * block, width)
    grad_rot = lax.dot_general(
        normed, grads, (((0,), (0,)), ((), ())), preferred_element_type=jnp.float32
    )
    return (kurt[:, :, :, 0].reshape(block), grad_rot / math.sqrt(4 * block))


def solution(mesh):
    fits = mesh.shape["tok"] == 4 and mesh.shape["col"] == 4
    return jax.shard_map(
        fused_shards if fits else shards,
        mesh=mesh,
        in_specs=(
            P(("groups", "tok"), "col"),
            P(("groups", "col"), "tok"),
            P("col", "tok"),
            P("tok"),
            P("tok", "col"),
        ),
        out_specs=(P(("groups", "tok")), P(("groups", "tok"), "col")),
        check_vma=False,
    )
```

```python
import functools
import math

import jax
import jax.numpy as jnp
from jax import lax
from jax.experimental import pallas as pl
from jax.experimental.pallas import tpu as pltpu
from jax.sharding import PartitionSpec as P

norm_eps = 1e-05
moment_eps = 1e-06


def kurtosis_terms(rotated, second, fourth, full_width):
    moment_two = second / full_width + moment_eps
    kurt_vals = fourth / full_width / (moment_two * moment_two)
    cubed = rotated * rotated * rotated
    grad_vals = (
        cubed / (moment_two * moment_two)[:, None] - (kurt_vals / moment_two)[:, None] * rotated
    )
    return (kurt_vals, grad_vals.astype(jnp.bfloat16))


def power_sums(rotated, along):
    squares = rotated * rotated
    return (jnp.sum(squares, axis=along), jnp.sum(squares * squares, axis=along))


def shards(attn_out, residual, w_out, norm_gain, rotation):
    heads_all = lax.all_gather(attn_out, "tok", axis=0, tiled=True)
    row_block = heads_all
    projected = lax.psum_scatter(
        jnp.dot(row_block, w_out, preferred_element_type=jnp.float32),
        "col",
        scatter_dimension=0,
        tiled=True,
    )
    hidden = residual.astype(jnp.float32) + projected
    square_sum = lax.psum(jnp.sum(hidden * hidden, axis=1), "tok")
    full_width = hidden.shape[1] * lax.axis_size("tok")
    row_scale = lax.rsqrt(square_sum / full_width + norm_eps)
    normed = (hidden * row_scale[:, None] * norm_gain[None, :]).astype(jnp.bfloat16)
    normed_all = lax.all_gather(normed, "col", axis=0, tiled=True)
    tokens_total = normed_all.shape[0]
    row_block = normed_all
    rotated = lax.psum_scatter(
        jnp.dot(row_block, rotation, preferred_element_type=jnp.float32),
        "tok",
        scatter_dimension=0,
        tiled=True,
    )
    second, fourth = lax.psum(power_sums(rotated, 1), "col")
    kurt_vals, grad_own = kurtosis_terms(rotated, second, fourth, full_width)
    grad_all = lax.all_gather(grad_own, "tok", axis=0, tiled=True)
    grad_rot = lax.dot_general(
        normed_all, grad_all, (((0,), (0,)), ((), ())), preferred_element_type=jnp.float32
    )
    return (kurt_vals, grad_rot / math.sqrt(tokens_total))


MESH = pl.DeviceIdType.MESH
block_order = (0, 2, 1, 3)
tile_cols = 256
row_step = 16
outer_rows = 256
outer_cols = 512


def rows_loop(count, body):
    def step(i, carry):
        body(pl.ds(pl.multiple_of(i * row_step, row_step), row_step))
        return carry

    lax.fori_loop(0, count // row_step, step, 0)


def kernel(
    full_width,
    attn_hbm, res_hbm, gain_hbm, w_hbm, rot_hbm,
    kurt_ref, norm_ref, grad_ref,
    res_ref, gain_ref, attn_all, w, rot, part, mate_buf, x_buf, rotp, z_buf, sumsq, stats,
    load_sem, ag_send, ag_recv, m_send, m_recv, x_send, x_recv, ss_send, ss_recv,
    n_send, n_recv, z_send, z_recv, st_send, st_recv, g_send, g_recv, k_send, k_recv, direct_send,
):
    g = lax.axis_index("groups")
    z = lax.axis_index("tok")
    c = lax.axis_index("col")
    core = lax.rem(c, 2)
    chip = lax.div(c, 2)
    mate = c + 1 - 2 * core
    across = lax.rem(c + 2, 4)
    block, width = attn_hbm.shape
    half = block // 2
    quarter = half // 2
    half_cols = width // 2

    def remote(src, dst, send, recv, to_z, to_c):
        return pltpu.make_async_remote_copy(
            src_ref=src, dst_ref=dst, send_sem=send, recv_sem=recv,
            device_id=(g, to_z, to_c), device_id_type=MESH,
        )

    def side(q):
        return pl.ds(q * half_cols, half_cols)

    load_attn = pltpu.make_async_copy(attn_hbm, attn_all.at[z], load_sem.at[0])
    load_w = [
        pltpu.make_async_copy(w_hbm.at[:, side(q)], w.at[:, side(q)], load_sem.at[1 + q])
        for q in (0, 1)
    ]
    load_rot = pltpu.make_async_copy(rot_hbm, rot, load_sem.at[3])
    load_res = pltpu.make_async_copy(res_hbm, res_ref, load_sem.at[4])
    load_gain = pltpu.make_async_copy(gain_hbm, gain_ref, load_sem.at[5])
    load_attn.start()
    load_w[0].start()
    load_w[1].start()

    barrier = pltpu.get_barrier_semaphore()
    for d in (1, 2, 3):
        pl.semaphore_signal(barrier, inc=1, device_id=(g, lax.rem(z + d, 4), c), device_id_type=MESH)
        pl.semaphore_signal(barrier, inc=1, device_id=(g, z, lax.rem(c + d, 4)), device_id_type=MESH)
    pl.semaphore_wait(barrier, 6)

    above = jnp.minimum(z + 1, 3)
    below = jnp.maximum(z - 1, 0)
    is_end = (z == 0) | (z == 3)
    is_mid = jnp.logical_not(is_end)

    def ag(s, up):
        return remote(
            attn_all.at[s], attn_all.at[s], ag_send.at[up, s], ag_recv.at[s],
            above if up else below, c,
        )

    def when(cond):
        return pl.when(cond)

    def ag_own(up):
        return remote(
            attn_hbm, attn_all.at[z], ag_send.at[up, z], ag_recv.at[z],
            above if up else below, c,
        )

    def ag_direct():
        return remote(
            attn_all.at[z], attn_all.at[z], direct_send.at[0], ag_recv.at[z], 3 - z, c
        )

    @when(z < 3)
    def _():
        ag_own(1).start()

    @when(z > 0)
    def _():
        ag_own(0).start()

    def tiles(left, left_at, right, out, q):
        def step(i, carry):
            cols = pl.ds(pl.multiple_of(q * half_cols + i * tile_cols, tile_cols), tile_cols)
            out[left_at, :, cols] = jnp.dot(
                left[left_at], right[:, cols], preferred_element_type=jnp.float32
            )
            return carry

        lax.fori_loop(0, half_cols // tile_cols, step, 0)

    def mate_copy(s, q):
        at = lax.div(s, 2)
        return remote(
            part.at[s, :, side(q)], mate_buf.at[at, :, side(q)], m_send.at[at, q],
            m_recv.at[at, q], z, mate,
        )

    def x_copy(s, q):
        return remote(
            part.at[s, :, side(q)], x_buf.at[:, side(q)], x_send.at[q], x_recv.at[q], z, across
        )

    def project(s, q):
        tiles(attn_all, s, w, part, q)

        @when(lax.rem(s, 2) != core)
        def _():
            mate_copy(s, q).start()

    def pair_sum(s, q):
        @when(lax.rem(s, 2) == core)
        def _():
            at = lax.div(s, 2)
            mate_copy(s, q).wait_recv()

            def add(rows):
                part[s, rows, side(q)] += mate_buf[at, rows, side(q)]

            rows_loop(block, add)

            @when(at != chip)
            def _():
                x_copy(s, q).start()

    first = jnp.where(z == 0, 1, z - 1)
    second = jnp.where(z == 0, 2, jnp.where(z == 3, 1, z + 1))
    third = jnp.where(z < 2, 3, 0)
    two_away = jnp.where(z < 2, z + 2, z - 2)

    load_attn.wait()
    load_w[0].wait()
    load_rot.start()
    load_res.start()
    load_gain.start()
    project(z, 0)

    @when(z > 0)
    def _():
        ag(below, 1).wait_recv()

        @when(z < 3)
        def _():
            ag(below, 1).start()

    @when(z < 3)
    def _():
        ag(above, 0).wait_recv()

        @when(z > 0)
        def _():
            ag(above, 0).start()

    @when(is_end)
    def _():
        ag_direct().start()

    load_w[1].wait()
    project(z, 1)
    pair_sum(z, 0)
    project(first, 0)
    pair_sum(z, 1)
    project(first, 1)
    pair_sum(first, 0)
    ag(two_away, 0).wait_recv()

    project(second, 0)
    pair_sum(first, 1)
    project(second, 1)
    pair_sum(second, 0)

    @when(is_end)
    def _():
        pair_sum(second, 1)
        ag(third, 0).wait_recv()

    project(third, 0)

    @when(is_mid)
    def _():
        pair_sum(second, 1)

    project(third, 1)
    pair_sum(third, 0)
    pair_sum(third, 1)

    load_res.wait()
    load_gain.wait()
    x_copy(c, 0).wait_recv()
    x_copy(c, 1).wait_recv()

    def add_residual(rows):
        hidden = res_ref[rows, :].astype(jnp.float32) + (part[c, rows, :] + x_buf[rows, :])
        part[c, rows, :] = hidden
        sumsq[z, rows, :] = jnp.broadcast_to(
            jnp.sum(hidden * hidden, axis=1, keepdims=True), (row_step, 128)
        )

    rows_loop(block, add_residual)

    def ss_copy(to_z):
        return remote(sumsq.at[z], sumsq.at[z], ss_send.at[to_z], ss_recv.at[z], to_z, c)

    def ss_arrival(from_z):
        return remote(
            sumsq.at[from_z], sumsq.at[from_z], ss_send.at[from_z], ss_recv.at[from_z], from_z, c
        )

    for d in (1, 2, 3):
        ss_copy(lax.rem(z + d, 4)).start()
    for d in (1, 2, 3):
        ss_arrival(lax.rem(z + d, 4)).wait_recv()

    def normalise(rows):
        total = sumsq[0, rows, :] + sumsq[1, rows, :] + sumsq[2, rows, :] + sumsq[3, rows, :]
        scale = lax.rsqrt(total / full_width + norm_eps)[:, :1]
        norm_ref[c, rows, :] = (part[c, rows, :] * scale * gain_ref[...]).astype(jnp.bfloat16)

    rows_loop(block, normalise)

    def norm_copy(b, at, to_c):
        return remote(norm_ref.at[b], norm_ref.at[b], n_send.at[at], n_recv.at[b], z, to_c)

    @when(core == 0)
    def _():
        norm_copy(c, 0, across).start()

    norm_copy(c, 1, mate).start()
    load_rot.wait()

    def rotate(b, q):
        if q == 0:

            @when(c != b)
            def _():
                norm_copy(b, 0, mate).wait_recv()

            @when(across == b)
            def _():
                norm_copy(b, 2, mate).start()

        tiles(norm_ref, b, rot, rotp, q)
        if b == block_order[0] and q == 0:

            @when(core == 1)
            def _():
                norm_copy(c, 0, across).start()


    def piece(h, q):
        return pl.ds(pl.multiple_of(h * half + q * quarter, quarter), quarter)

    def z_copy(u, h, to_z):
        b, q = u
        return remote(
            rotp.at[b, piece(h, q)], z_buf.at[b, h, q], z_send.at[b, h, q], z_recv.at[b, h, q],
            to_z, c,
        )

    def g_copy(u, h, to_z):
        b, q = u
        return remote(
            grad_ref.at[b, piece(h, q)], grad_ref.at[b, piece(h, q)], g_send.at[b, h, q],
            g_recv.at[b, h, q], to_z, c,
        )

    def chain_add(u, h):
        b, q = u
        z_copy(u, h, below).wait_recv()
        rotp[b, piece(h, q), :] += z_buf[b, h, q]

    out_half = jnp.where(z == 0, 1, 0)
    in_half = 1 - out_half
    inner = jnp.where(z == 0, 1, 2)
    near = jnp.where(z == 1, 1, 0)
    far = 1 - near
    end_z = jnp.where(z == 1, 0, 3)
    other_mid = jnp.where(z == 1, 2, 1)
    units = [(b, q) for b in block_order for q in (0, 1)]
    last = len(units)

    def near_step(i):
        if 0 <= i < last:
            chain_add(units[i], near)
            z_copy(units[i], near, other_mid).start()

    def far_step(i):
        if 0 <= i < last:
            chain_add(units[i], far)
            z_copy(units[i], far, end_z).start()

    def stat_copy(u, to_c):
        b, q = u
        return remote(
            stats.at[b, q, c], stats.at[b, q, c], st_send.at[b, q, to_c], st_recv.at[b, q, c],
            z, to_c,
        )

    def stat_arrival(u, from_c):
        b, q = u
        return remote(
            stats.at[b, q, from_c], stats.at[b, q, from_c], st_send.at[b, q, from_c],
            st_recv.at[b, q, from_c], z, from_c,
        )

    def kurt_copy(u):
        b, q = u
        return remote(
            stats.at[b, q, 4, 0], kurt_ref.at[in_half, q], k_send.at[b, q], k_recv.at[in_half, q],
            jnp.int32(b), c,
        )

    def moments(u):
        b, q = u
        chain_add(u, in_half)
        squares = rotp[b, piece(in_half, q), :]
        squares = squares * squares
        stats[b, q, c, 0] = jnp.broadcast_to(
            jnp.sum(squares, axis=1, keepdims=True), (quarter, 128)
        )
        stats[b, q, c, 1] = jnp.broadcast_to(
            jnp.sum(squares * squares, axis=1, keepdims=True), (quarter, 128)
        )
        for d in (1, 2, 3):
            stat_copy(u, lax.rem(c + d, 4)).start()

    def finish(u):
        b, q = u
        for d in (1, 2, 3):
            stat_arrival(u, lax.rem(c + d, 4)).wait_recv()
        sums = [
            stats[b, q, 0, p] + stats[b, q, 1, p] + stats[b, q, 2, p] + stats[b, q, 3, p]
            for p in (0, 1)
        ]
        moment = sums[0] / full_width + moment_eps
        squared = moment * moment
        kurt = sums[1] / full_width / squared
        stats[b, q, 4, 0] = kurt
        cubic = (1.0 / squared)[:, :1]
        linear = (kurt / moment)[:, :1]
        rotated = rotp[b, piece(in_half, q), :]
        grad_ref[b, piece(in_half, q), :] = (
            rotated * rotated * rotated * cubic - linear * rotated
        ).astype(jnp.bfloat16)
        g_copy(u, in_half, inner).start()

        @when(z != b)
        def _():
            kurt_copy(u).start()

        if b in (0, 3):

            @when(z == b)
            def _():
                kurt_ref[in_half, q] = kurt

    def near_grad(i):
        if 0 <= i < last:
            g_copy(units[i], far, other_mid).wait_recv()
            g_copy(units[i], far, other_mid).start()

    def far_grad(i):
        if 0 <= i < last:
            g_copy(units[i], near, end_z).wait_recv()
            g_copy(units[i], near, end_z).start()

    @when(is_end)
    def _():
        for b in block_order:
            rotate(b, 0)
            rotate(b, 1)
            for q in (0, 1):
                z_copy((b, q), out_half, inner).start()
        for i, u in enumerate(units):
            moments(u)
            if i > 0:
                finish(units[i - 1])
        finish(units[-1])
        for u in units:
            g_copy(u, out_half, inner).wait_recv()

    @when(is_mid)
    def _():
        for b in block_order[:2]:
            rotate(b, 0)
            rotate(b, 1)
        later = [(b, q) for b in block_order[2:] for q in (0, 1)]
        for i in range(last + 8):
            near_step(i)
            far_step(i - 1)
            near_grad(i - 6)
            far_grad(i - 7)
            if i < len(later):
                rotate(*later[i])

    def kurt_arrival(h, q):
        return remote(
            stats.at[0, q, 4, 0], kurt_ref.at[h, q], k_send.at[0, q], k_recv.at[h, q],
            jnp.int32(3 * h), c,
        )

    for q in (0, 1):

        @when(z != 0)
        def _():
            kurt_arrival(0, q).wait_recv()

        @when(z != 3)
        def _():
            kurt_arrival(1, q).wait_recv()

    for s in range(4):

        @when((s <= z) & (s >= z - 1) & (z < 3))
        def _():
            ag(s, 1).wait_send()

        @when((s >= z) & (s <= z + 1) & (z > 0))
        def _():
            ag(s, 0).wait_send()

        for q in (0, 1):

            @when(core != s % 2)
            def _():
                mate_copy(jnp.int32(s), q).wait_send()

            u = (s, q)

            @when(is_mid)
            def _():
                for h in (0, 1):
                    z_copy(u, h, below).wait_send()
                    g_copy(u, h, below).wait_send()

            @when(is_end)
            def _():
                z_copy(u, out_half, inner).wait_send()
                g_copy(u, in_half, inner).wait_send()
                for d in (1, 2, 3):
                    stat_copy(u, lax.rem(c + d, 4)).wait_send()

                @when(z != s)
                def _():
                    kurt_copy(u).wait_send()

    @when(is_end)
    def _():
        ag_direct().wait_send()

    for q in (0, 1):
        x_copy(across, q).wait_send()
    for d in (1, 2, 3):
        ss_copy(lax.rem(z + d, 4)).wait_send()
    norm_copy(c, 0, across).wait_send()
    norm_copy(c, 1, mate).wait_send()
    norm_copy(across, 2, mate).wait_send()


def outer(root, norm_ref, grad_ref, kurt_ref, out_ref, kurt_row):
    @pl.when(pl.program_id(0) == 0)
    def _():
        shape = kurt_ref.shape
        on_diagonal = lax.broadcasted_iota(jnp.int32, shape, 0) == lax.broadcasted_iota(
            jnp.int32, shape, 1
        )
        row = jnp.sum(jnp.where(on_diagonal, kurt_ref[...], 0.0), axis=0, keepdims=True)
        kurt_row[...] = row[:, : kurt_row.shape[1]]

    for i in range(out_ref.shape[1] // outer_cols):
        cols = pl.ds(i * outer_cols, outer_cols)
        out_ref[:, cols] = (
            lax.dot_general(
                norm_ref[...], grad_ref[:, cols], (((0,), (0,)), ((), ())),
                preferred_element_type=jnp.float32,
            )
            / root
        )


def fused_shards(attn_out, residual, w_out, norm_gain, rotation):
    block, width = attn_out.shape
    full_width = width * 4
    quarter = block // 4
    dma = pltpu.SemaphoreType.DMA
    vmem = pl.BlockSpec(memory_space=pltpu.VMEM)
    kurt, normed, grads = pl.pallas_call(
        functools.partial(kernel, full_width),
        out_shape=(
            jax.ShapeDtypeStruct((2, 2, quarter, 128), jnp.float32),
            jax.ShapeDtypeStruct((4, block, width), jnp.bfloat16),
            jax.ShapeDtypeStruct((4, block, width), jnp.bfloat16),
        ),
        in_specs=[pl.BlockSpec(memory_space=pltpu.HBM)] * 5,
        out_specs=(vmem, vmem, vmem),
        scratch_shapes=[
            pltpu.VMEM((block, width), jnp.bfloat16),
            pltpu.VMEM((1, width), jnp.float32),
            pltpu.VMEM((4, block, width), jnp.bfloat16),
            pltpu.VMEM(w_out.shape, jnp.bfloat16),
            pltpu.VMEM(rotation.shape, jnp.bfloat16),
            pltpu.VMEM((4, block, width), jnp.float32),
            pltpu.VMEM((2, block, width), jnp.float32),
            pltpu.VMEM((block, width), jnp.float32),
            pltpu.VMEM((4, block, width), jnp.float32),
            pltpu.VMEM((4, 2, 2, quarter, width), jnp.float32),
            pltpu.VMEM((4, block, 128), jnp.float32),
            pltpu.VMEM((4, 2, 5, 2, quarter, 128), jnp.float32),
            dma((6,)), dma((2, 4)), dma((4,)), dma((2, 2)), dma((2, 2)), dma((2,)), dma((2,)),
            dma((4,)), dma((4,)), dma((3,)), dma((4,)), dma((4, 2, 2)), dma((4, 2, 2)),
            dma((4, 2, 4)), dma((4, 2, 4)), dma((4, 2, 2)), dma((4, 2, 2)), dma((4, 2)), dma((2, 2)),
            dma((1,)),
        ],
        compiler_params=pltpu.CompilerParams(
            collective_id=0, has_side_effects=True, vmem_limit_bytes=60 * 1024 * 1024
        ),
    )(attn_out, residual, norm_gain.reshape(1, width), w_out, rotation)
    tokens = 4 * block
    grad_rot, kurt_row = pl.pallas_call(
        functools.partial(outer, math.sqrt(tokens)),
        grid=(width // outer_rows,),
        out_shape=(
            jax.ShapeDtypeStruct((width, width), jnp.float32),
            jax.ShapeDtypeStruct((1, block), jnp.float32),
        ),
        in_specs=[
            pl.BlockSpec((tokens, outer_rows), lambda i: (0, i)),
            pl.BlockSpec((tokens, width), lambda i: (0, 0)),
            pl.BlockSpec((block, 128), lambda i: (0, 0)),
        ],
        out_specs=(
            pl.BlockSpec((outer_rows, width), lambda i: (i, 0)),
            pl.BlockSpec((1, block), lambda i: (0, 0)),
        ),
        cost_estimate=pl.CostEstimate(
            flops=2 * tokens * width * width, bytes_accessed=4 * width * width, transcendentals=0
        ),
    )(normed.reshape(tokens, width), grads.reshape(tokens, width), kurt.reshape(block, 128))
    return (kurt_row.reshape(block), grad_rot)


def solution(mesh):
    fits = mesh.shape["tok"] == 4 and mesh.shape["col"] == 4
    return jax.shard_map(
        fused_shards if fits else shards,
        mesh=mesh,
        in_specs=(
            P(("groups", "tok"), "col"),
            P(("groups", "col"), "tok"),
            P("col", "tok"),
            P("tok"),
            P("tok", "col"),
        ),
        out_specs=(P(("groups", "tok")), P(("groups", "tok"), "col")),
        check_vma=False,
    )
```
